256 devices in a mesh: row: 2 (over core), col: 16 (over y, x), depth: 8 (over z).
Axes of the slice: x: 4, y: 4, z: 8, core: 2. Of those that a mesh axis runs over, the one named last changes fastest.
Arguments:
- tensor: bfloat16 [4096, 128, 2048], P(('row', 'col', 'depth')), may hold values from -6 to 6
- density: bfloat16 [4096, 1024], P(('row', 'col', 'depth')), may hold values from -0.09375 to 0.09375
- tensor_mask: int32 [64, 2, 32], replicated, may hold values 0 or 1
- density_mask: int32 [64, 16], replicated, may hold values 0 or 1
Outputs:
- contracted: bfloat16 [1024, 128, 2048], P('depth', 'row', 'col')
The draws below stay inside these ranges and needn't reach their ends.
All inputs are finite; a program needn't handle non-finite values.
Results may differ from the reference program's by a relative error of at most 0.017.
Values may be sent and summed in bfloat16 or wider, within the bound.
A program may use at most 192 MiB of HBM per device.

```python
import jax
import jax.numpy as jnp
from jax import lax

BLK = 64
NU_DEV = 16
NNU = 4096
NMU = 128
NAUX = 2048
NSIG = 1024
N_DEPTH = 8


def set_ends(values, key, smallest, high):
    index_at = [jax.random.randint(jax.random.fold_in(key, axis), (), 0, length) for axis, length in enumerate(values.shape)]
    longest = values.shape.index(max(values.shape))
    beside = index_at[:longest] + [(index_at[longest] + 1) % values.shape[longest]] + index_at[longest + 1:]
    return values.at[tuple(index_at)].set(smallest).at[tuple(beside)].set(high)


def block_scale(own_key, dims, cuts, low, top_value):
    level, own = 1.0, jax.random.fold_in(own_key, 6)
    for axis_at, shards_of in cuts:
        steps = jnp.exp(jax.random.uniform(jax.random.fold_in(own, axis_at), (shards_of,), jnp.float32, low / len(cuts), top_value / len(cuts)))
        level = level * jnp.repeat(steps, dims[axis_at] // shards_of).reshape([-1 if axis == axis_at else 1 for axis in range(len(dims))])
    return level


def scatter_about(rng, dims, width, most, cuts=(), kind=jnp.bfloat16):
    level = block_scale(rng, dims, cuts, -0.22, 0.18) if cuts else 1.0
    drawn = jax.random.normal(rng, dims, jnp.float32) * width * level
    return jnp.minimum(jnp.maximum(drawn, -most), most).astype(kind)


def setup_inputs(seed: int = 0) -> dict:
    key_of = jax.random.split(jax.random.key(seed), 5)
    return {
        "tensor": scatter_about(key_of[0], (NNU, NMU, NAUX), 1.0, 6.0, ((0, 256),)),
        "density": scatter_about(key_of[1], (NNU, NSIG), NNU ** -0.5, 0.09375, ((0, 256),)),
        "tensor_mask": set_ends((jax.random.randint(key_of[2], (NNU // BLK, NMU // BLK, NAUX // BLK), 0, 4) < 3).astype(jnp.int32), jax.random.fold_in(key_of[2], 1), 0, 1),
        "density_mask": set_ends((jax.random.randint(key_of[3], (NNU // BLK, NSIG // BLK), 0, 4) < 3).astype(jnp.int32), jax.random.fold_in(key_of[3], 1), 0, 1),
    }


def reference(tensor, density, tensor_mask, density_mask):
    nu_total, mu_total, aux_total = tensor.shape
    sigma_total = density.shape[1]
    groups = nu_total // (NU_DEV * N_DEPTH)
    density_keep = jnp.repeat(jnp.repeat(density_mask, BLK, axis=0), BLK, axis=1).astype(density.dtype)
    density_kept = (density * density_keep).astype(jnp.float32).reshape(groups, N_DEPTH, NU_DEV, sigma_total)
    row_keep = jnp.repeat(tensor_mask, BLK, axis=0)

    def one_block(block_index):
        mu_slab = lax.dynamic_slice_in_dim(tensor, block_index * BLK, BLK, 1)
        keep_mask = lax.dynamic_slice_in_dim(row_keep, block_index, 1, 1)
        keep_mask = jnp.repeat(keep_mask, BLK, axis=2).astype(mu_slab.dtype)
        mu_slab = (mu_slab * keep_mask).astype(jnp.float32).reshape(groups, N_DEPTH, NU_DEV, BLK, aux_total)
        partial_value = jnp.einsum("gdumq,gdus->dsmq", mu_slab, density_kept, precision=lax.Precision.HIGHEST)
        rounded = lax.optimization_barrier(partial_value.astype(jnp.bfloat16))
        return jnp.sum(rounded.astype(jnp.float32), axis=0).astype(jnp.bfloat16)

    blocks = lax.map(one_block, jnp.arange(mu_total // BLK, dtype=jnp.int32))
    return jnp.transpose(blocks, (1, 0, 2, 3)).reshape(sigma_total, mu_total, aux_total)
```

```python
import functools

import jax
import jax.numpy as jnp
from jax import lax
from jax.experimental import pallas as pl
from jax.experimental.pallas import tpu as pltpu
from jax.sharding import PartitionSpec as P

BLK = 64
MESH = pl.DeviceIdType.MESH
MC = 4
GROUP = 16
BF, F32 = jnp.bfloat16, jnp.float32


def kernel(
    n_row, n_col, n_dep, tensor, density, tmask, dmask, out,
    raw, wide, ready, cols, down, up, first, own_den, den, den_t, total,
    load_sem, den_send, den_recv, x_send, x_recv, z_send, z_recv,
):
    nu, _, mu, aux = tensor.shape
    sigma = density.shape[1]
    per_dev = sigma // n_dep
    half_rows = per_dev // 2
    q_dev = aux // n_col
    chunks = mu // MC
    per_group = GROUP // MC
    hops = n_dep // 2
    peers = n_row * n_col
    row, col, dep = lax.axis_index("row"), lax.axis_index("col"), lax.axis_index("depth")
    me = row * n_col + col
    left, right = lax.rem(dep + n_dep - 1, n_dep), lax.rem(dep + 1, n_dep)
    nu_block = lax.div((me * n_dep + dep) * nu, BLK)
    low = lax.broadcasted_iota(jnp.int32, (nu, 128), 1) < BLK

    def peer(p):
        off = lax.rem(lax.div(p, 2) * 7, n_col)
        pr = lax.rem(row + lax.rem(p, 2), 2)
        y = lax.rem(lax.div(col, 4) + lax.div(off, 4), 4)
        x = lax.rem(lax.rem(col, 4) + lax.rem(off, 4), 4)
        return pr, y * 4 + x

    def load(g):
        return pltpu.make_async_copy(tensor.at[:, :, pl.ds(pl.multiple_of(g * GROUP, GROUP), GROUP), :], raw, load_sem)

    load(0).start()

    for j in range(sigma // 128):
        a = dmask[nu_block, 2 * j].astype(F32)
        b = dmask[nu_block, 2 * j + 1].astype(F32)
        lanes = slice(j * 128, (j + 1) * 128)
        own_den[:, lanes] = (density[:, lanes].astype(F32) * jnp.where(low, a, b)).astype(BF)

    barrier = pltpu.get_barrier_semaphore()

    @pl.loop(1, peers)
    def _(p):
        pr, pc = peer(p)
        pl.semaphore_signal(barrier, inc=1, device_id=(pr, pc, dep), device_id_type=MESH)

    pl.semaphore_signal(barrier, inc=1, device_id=(row, col, left), device_id_type=MESH)
    pl.semaphore_signal(barrier, inc=1, device_id=(row, col, right), device_id_type=MESH)
    pl.semaphore_wait(barrier, peers + 1)

    mine = pl.ds(pl.multiple_of(me * nu, nu), nu)
    pltpu.make_async_copy(own_den, den.at[mine], den_recv).start()

    @pl.loop(1, peers)
    def _(p):
        pr, pc = peer(p)
        pltpu.make_async_remote_copy(
            own_den, den.at[mine], den_send, den_recv, device_id=(pr, pc, dep), device_id_type=MESH
        ).start()

    def prepare(k):
        @pl.when(lax.rem(k, per_group) == 0)
        def _():
            g = lax.div(k, per_group)
            load(g).wait()

            @pl.loop(0, n_col)
            def _(c):
                lanes = pl.ds(pl.multiple_of(c * q_dev, q_dev), q_dev)
                for h in range(n_row):
                    a = tmask[nu_block, h, 2 * c].astype(F32)
                    b = tmask[nu_block, h, 2 * c + 1].astype(F32)
                    keep = jnp.where(low, a, b)[:1][None]
                    part = raw[:, h, :, lanes].astype(F32) * keep
                    wide[h, c] = part.reshape(nu * GROUP, q_dev)

            @pl.when(g + 1 < mu // GROUP)
            def _():
                load(g + 1).start()

        at = lax.rem(k, per_group) * MC

        @pl.loop(0, n_col)
        def _(c):
            for h in range(n_row):
                for j in range(MC):
                    ready[k, h, c, :, j * q_dev : (j + 1) * q_dev] = wide[
                        h, c, pl.ds(at + j, nu, stride=GROUP), :
                    ].astype(BF)

        pltpu.make_async_copy(ready.at[k, row, col], cols.at[k, mine], x_recv.at[k]).start()

        @pl.loop(1, peers)
        def _(p):
            pr, pc = peer(p)
            pltpu.make_async_remote_copy(
                ready.at[k, pr, pc], cols.at[k, mine], x_send.at[k], x_recv.at[k],
                device_id=(pr, pc, dep), device_id_type=MESH,
            ).start()

    def product(k, ahead):
        target = lax.rem(dep + ahead + n_dep, n_dep)
        rows = pl.ds(pl.multiple_of(target * per_dev, per_dev), per_dev)
        return jnp.dot(den_t[rows, :], cols[k], preferred_element_type=F32)

    ways = ((down, right, 1), (up, left, -1))

    def rows_of(w, t):
        if t:
            return slice(None)
        return pl.ds(w * half_rows, half_rows)

    def hop(w, k, t):
        buf, other, _ = ways[w]
        rows = rows_of(w, t)
        src = first.at[k, rows] if t == 0 else buf.at[k, t - 1]
        return pltpu.make_async_remote_copy(
            src, buf.at[k, t, rows], z_send.at[w, k, t], z_recv.at[w, k, t],
            device_id=(row, col, other), device_id_type=MESH,
        )

    def stage(k, t):
        if t == 0:
            pltpu.make_async_copy(cols.at[k], cols.at[k], x_recv.at[k]).wait()
            first[k] = product(k, hops).astype(BF)
            for w in range(2):
                hop(w, k, 0).start()
        elif t < hops:
            for w in range(2):
                buf, _, sign = ways[w]
                mult = product(k, sign * (hops - t))
                hop(w, k, t - 1).wait_recv()
                if t == 1:
                    lo, hi = slice(0, half_rows), slice(half_rows, per_dev)
                    got, fresh = (lo, hi) if w == 0 else (hi, lo)
                    buf[k, 0, got] = (mult[got] + buf[k, 0, got].astype(F32)).astype(BF)
                    buf[k, 0, fresh] = mult[fresh].astype(BF)
                else:
                    buf[k, t - 1] = (mult + buf[k, t - 1].astype(F32)).astype(BF)
                hop(w, k, t).start()
        else:
            mult = product(k, 0)
            for w in range(2):
                hop(w, k, t - 1).wait_recv()
            mult = mult + down[k, t - 1].astype(F32) + up[k, t - 1].astype(F32)
            at = lax.rem(k, per_group) * MC
            for j in range(MC):
                total[pl.ds(at + j, per_dev, stride=GROUP), :] = mult[:, j * q_dev : (j + 1) * q_dev]

            @pl.when(lax.rem(k, per_group) == per_group - 1)
            def _():
                g = pl.ds(pl.multiple_of(lax.div(k, per_group) * GROUP, GROUP), GROUP)

                @pl.loop(0, per_dev // 16)
                def _(s):
                    part = total[pl.ds(pl.multiple_of(s * 16 * GROUP, 16 * GROUP), 16 * GROUP), :]
                    out[pl.ds(s * 16, 16), g, :] = part.reshape(16, GROUP, q_dev).astype(BF)

    prepare(0)
    prepare(1)
    pltpu.make_async_copy(den, den, den_recv).wait()

    @pl.loop(0, n_dep)
    def _(j):
        at = pl.ds(pl.multiple_of(j * per_dev, per_dev), per_dev)
        den_t[at, :] = den[:, at].astype(F32).T.astype(BF)

    @pl.loop(0, chunks + hops)
    def _(i):
        for t in range(hops, -1, -1):
            if t == 0:
                @pl.when(i + 2 < chunks)
                def _():
                    prepare(i + 2)

            @pl.when((i - t >= 0) & (i - t < chunks))
            def _(t=t):
                stage(i - t, t)

    others = pl.ds(0, (peers - 1) * nu)
    pltpu.make_async_copy(den.at[others], den.at[others], den_send).wait()

    @pl.loop(0, chunks)
    def _(k):
        pltpu.make_async_copy(cols.at[k, others], cols.at[k, others], x_send.at[k]).wait()
        for w in range(2):
            for t in range(hops):
                hop(w, k, t).wait_send()


def solution(mesh):
    n_row, n_col, n_dep = (mesh.shape[a] for a in ("row", "col", "depth"))

    def body(tensor, density, tensor_mask, density_mask):
        nu, mu_all, aux = tensor.shape
        sigma = density.shape[1]
        mu, q_dev, per_dev = mu_all // n_row, aux // n_col, sigma // n_dep
        chunks, hops, plane, width = mu // MC, n_dep // 2, nu * n_row * n_col, MC * (aux // n_col)
        vmem, smem = pl.BlockSpec(memory_space=pltpu.VMEM), pl.BlockSpec(memory_space=pltpu.SMEM)
        return pl.pallas_call(
            functools.partial(kernel, n_row, n_col, n_dep),
            out_shape=jax.ShapeDtypeStruct((per_dev, mu, q_dev), BF),
            in_specs=[pl.BlockSpec(memory_space=pl.ANY), vmem, smem, smem],
            out_specs=vmem,
            scratch_shapes=[
                pltpu.VMEM((nu, n_row, GROUP, aux), BF),
                pltpu.VMEM((n_row, n_col, nu * GROUP, q_dev), F32),
                pltpu.VMEM((chunks, n_row, n_col, nu, width), BF),
                pltpu.VMEM((chunks, plane, width), BF),
                pltpu.VMEM((chunks, hops, per_dev, width), BF),
                pltpu.VMEM((chunks, hops, per_dev, width), BF),
                pltpu.VMEM((chunks, per_dev, width), BF),
                pltpu.VMEM((nu, sigma), BF),
                pltpu.VMEM((plane, sigma), BF),
                pltpu.VMEM((sigma, plane), BF),
                pltpu.VMEM((per_dev * GROUP, q_dev), F32),
                pltpu.SemaphoreType.DMA,
                pltpu.SemaphoreType.DMA,
                pltpu.SemaphoreType.DMA,
                pltpu.SemaphoreType.DMA((chunks,)),
                pltpu.SemaphoreType.DMA((chunks,)),
                pltpu.SemaphoreType.DMA((2, chunks, hops)),
                pltpu.SemaphoreType.DMA((2, chunks, hops)),
            ],
            compiler_params=pltpu.CompilerParams(
                collective_id=0, has_side_effects=True, vmem_limit_bytes=58 << 20
            ),
        )(tensor.reshape(nu, n_row, mu, aux), density, tensor_mask, density_mask)

    placed = (P(("row", "col", "depth"), None, None), P(("row", "col", "depth"), None), P(), P())
    return jax.shard_map(
        body, mesh=mesh, in_specs=placed, out_specs=P("depth", "row", "col"), check_vma=False
    )
```

```python
import functools

import jax
import jax.numpy as jnp
from jax import lax
from jax.experimental import pallas as pl
from jax.experimental.pallas import tpu as pltpu
from jax.sharding import PartitionSpec as P

BLK = 64
MESH = pl.DeviceIdType.MESH
MC = 4
GROUP = 16
LEAD = 2
BF, F32 = jnp.bfloat16, jnp.float32


def kernel(
    n_row, n_col, n_dep, tensor, density, tmask, dmask, out,
    raw, wide, ready, cols, down, up, first, own_den, den, den_t, total,
    load_sem, den_send, den_recv, sib_send, sib_recv, x_send, x_recv, z_send, z_recv,
):
    nu, _, mu, aux = tensor.shape
    per_dev = den.shape[2]
    half_rows = per_dev // 2
    q_dev = aux // n_col
    chunks = mu // MC
    per_group = GROUP // MC
    hops = n_dep // 2
    peers = n_row * n_col
    row, col, dep = lax.axis_index("row"), lax.axis_index("col"), lax.axis_index("depth")
    me = row * n_col + col
    left, right = lax.rem(dep + n_dep - 1, n_dep), lax.rem(dep + 1, n_dep)
    nu_block = lax.div((me * n_dep + dep) * nu, BLK)
    low = lax.broadcasted_iota(jnp.int32, (nu, 128), 1) < BLK
    mine = pl.ds(pl.multiple_of(me * nu, nu), nu)
    same_core = pl.ds(pl.multiple_of(row * n_col * nu, n_col * nu), n_col * nu)

    def peer(p):
        off = lax.rem(lax.div(p, 2) * 7, n_col)
        pr = lax.rem(row + lax.rem(p, 2), 2)
        y = lax.rem(lax.div(col, 4) + lax.div(off, 4), 4)
        x = lax.rem(lax.rem(col, 4) + lax.rem(off, 4), 4)
        return pr, y * 4 + x


    def load(g):
        return pltpu.make_async_copy(tensor.at[:, :, pl.ds(pl.multiple_of(g * GROUP, GROUP), GROUP), :], raw, load_sem)

    def widen(g):
        load(g).wait()

        @pl.loop(0, n_col)
        def _(c):
            lanes = pl.ds(pl.multiple_of(c * q_dev, q_dev), q_dev)
            for h in range(n_row):
                a = tmask[h, 2 * c, nu_block].astype(F32)
                b = tmask[h, 2 * c + 1, nu_block].astype(F32)
                keep = jnp.where(low, a, b)[:1][None]
                part = raw[:, h, :, lanes].astype(F32) * keep
                wide[h, c] = part.reshape(nu * GROUP, q_dev)

    def arrange(k):
        at = lax.rem(k, per_group) * MC

        @pl.loop(0, n_col)
        def _(c):
            for h in range(n_row):
                for j in range(MC):
                    ready[k, h, c, :, j * q_dev : (j + 1) * q_dev] = wide[
                        h, c, pl.ds(at + j, nu, stride=GROUP), :
                    ].astype(BF)

    def send(k):
        pltpu.make_async_copy(ready.at[k, row, col], cols.at[k, mine], x_recv.at[k]).start()

        @pl.loop(1, peers)
        def _(p):
            pr, pc = peer(p)
            pltpu.make_async_remote_copy(
                ready.at[k, pr, pc], cols.at[k, mine], x_send.at[k], x_recv.at[k],
                device_id=(pr, pc, dep), device_id_type=MESH,
            ).start()

    def prepare(k):
        @pl.when(lax.rem(k, per_group) == 0)
        def _():
            g = lax.div(k, per_group)
            widen(g)

            @pl.when(g + 1 < mu // GROUP)
            def _():
                load(g + 1).start()

        arrange(k)
        send(k)


    aheads = [hops] + [s * a for a in range(hops - 1, 0, -1) for s in (1, -1)] + [0]
    needs = [[0]] + [[2 * t - 1, 2 * t] for t in range(1, hops)] + [[n_dep - 1]]

    def block_of(ahead):
        return lax.rem(dep + ahead + n_dep, n_dep)

    def send_den(n):
        b = block_of(aheads[n])
        pltpu.make_async_copy(own_den.at[b], den.at[b, mine], den_recv.at[n]).start()

        @pl.loop(1, n_col)
        def _(p):
            _, pc = peer(2 * p)
            pltpu.make_async_remote_copy(
                own_den.at[b], den.at[b, mine], den_send.at[n], den_recv.at[n],
                device_id=(row, pc, dep), device_id_type=MESH,
            ).start()

    def sibling(n):
        part = den.at[block_of(aheads[n]), same_core]
        return pltpu.make_async_remote_copy(
            part, part, sib_send.at[n], sib_recv.at[n], device_id=(1 - row, col, dep), device_id_type=MESH
        )

    def share_den(n):
        part = den.at[block_of(aheads[n]), same_core]
        pltpu.make_async_copy(part, part, den_recv.at[n]).wait()
        sibling(n).start()

    def turn_den(n):
        b = block_of(aheads[n])
        sibling(n).wait_recv()
        den_t[b] = den[b].astype(F32).T.astype(BF)


    def product(k, ahead):
        return jnp.dot(den_t[block_of(ahead)], cols[k], preferred_element_type=F32)

    ways = ((down, right, 1), (up, left, -1))

    def hop(w, k, t):
        buf, other, _ = ways[w]
        rows = pl.ds(w * half_rows, half_rows) if t == 0 else slice(None)
        src = first.at[k, rows] if t == 0 else buf.at[k, t - 1]
        return pltpu.make_async_remote_copy(
            src, buf.at[k, t, rows], z_send.at[w, k], z_recv.at[w, k, t],
            device_id=(row, col, other), device_id_type=MESH,
        )

    def sent(k):
        rest = pl.ds(0, (peers - 1) * nu)
        pltpu.make_async_copy(cols.at[k, rest], cols.at[k, rest], x_send.at[k]).wait()
        rest = pl.ds(0, hops * per_dev - half_rows)
        for w in range(2):
            pltpu.make_async_copy(cols.at[k, rest], cols.at[k, rest], z_send.at[w, k]).wait()

    def stage(k, t):
        if t == 0:
            pltpu.make_async_copy(cols.at[k], cols.at[k], x_recv.at[k]).wait()
            first[k] = product(k, hops).astype(BF)
            for w in range(2):
                hop(w, k, 0).start()
        elif t < hops:
            for w in range(2):
                buf, _, sign = ways[w]
                mult = product(k, sign * (hops - t))
                hop(w, k, t - 1).wait_recv()
                if t == 1:
                    lo, hi = slice(0, half_rows), slice(half_rows, per_dev)
                    got, fresh = (lo, hi) if w == 0 else (hi, lo)
                    buf[k, 0, got] = (mult[got] + buf[k, 0, got].astype(F32)).astype(BF)
                    buf[k, 0, fresh] = mult[fresh].astype(BF)
                else:
                    buf[k, t - 1] = (mult + buf[k, t - 1].astype(F32)).astype(BF)
                hop(w, k, t).start()
        else:
            mult = product(k, 0)
            for w in range(2):
                hop(w, k, t - 1).wait_recv()
            mult = mult + down[k, t - 1].astype(F32) + up[k, t - 1].astype(F32)
            at = lax.rem(k, per_group) * MC
            for j in range(MC):
                total[pl.ds(at + j, per_dev, stride=GROUP), :] = mult[:, j * q_dev : (j + 1) * q_dev]

            @pl.when(lax.rem(k, per_group) == per_group - 1)
            def _():
                g = pl.ds(pl.multiple_of(lax.div(k, per_group) * GROUP, GROUP), GROUP)

                @pl.loop(0, per_dev // 16)
                def _(s):
                    part = total[pl.ds(pl.multiple_of(s * 16 * GROUP, 16 * GROUP), 16 * GROUP), :]
                    out[pl.ds(s * 16, 16), g, :] = part.reshape(16, GROUP, q_dev).astype(BF)

            @pl.when(k > 0)
            def _():
                sent(k - 1)

    load(0).start()
    for j in range(n_dep * per_dev // 128):
        a = dmask[2 * j, nu_block].astype(F32)
        b = dmask[2 * j + 1, nu_block].astype(F32)
        at = slice(j * 128 % per_dev, j * 128 % per_dev + 128)
        own_den[j * 128 // per_dev, :, at] = (
            density[:, j * 128 : (j + 1) * 128].astype(F32) * jnp.where(low, a, b)
        ).astype(BF)
    widen(0)
    load(1).start()
    for k in range(LEAD):
        arrange(k)

    barrier = pltpu.get_barrier_semaphore()

    @pl.loop(1, peers)
    def _(p):
        pr, pc = peer(p)
        pl.semaphore_signal(barrier, inc=1, device_id=(pr, pc, dep), device_id_type=MESH)

    pl.semaphore_signal(barrier, inc=1, device_id=(row, col, left), device_id_type=MESH)
    pl.semaphore_signal(barrier, inc=1, device_id=(row, col, right), device_id_type=MESH)
    pl.semaphore_wait(barrier, peers + 1)

    for k in range(LEAD):
        for n in needs[k]:
            send_den(n)
        send(k)
    for n in needs[0]:
        share_den(n)

    @pl.loop(0, chunks + hops)
    def _(i):
        for t in range(hops, -1, -1):
            if t == 0:
                for s in range(LEAD, hops + 1):
                    @pl.when(i == s - LEAD)
                    def _(s=s):
                        for n in needs[s]:
                            send_den(n)

                @pl.when(i + LEAD < chunks)
                def _():
                    prepare(i + LEAD)

            @pl.when(i == t)
            def _(t=t):
                for n in needs[t]:
                    turn_den(n)

            @pl.when((i - t >= 0) & (i - t < chunks))
            def _(t=t):
                stage(i - t, t)

        for s in range(1, hops + 1):
            @pl.when(i == s - 1)
            def _(s=s):
                for n in needs[s]:
                    share_den(n)

    sent(chunks - 1)
    rest = pl.ds(0, (n_col - 1) * nu)
    for n in range(n_dep):
        pltpu.make_async_copy(den.at[0, rest], den.at[0, rest], den_send.at[n]).wait()
        sibling(n).wait_send()


def solution(mesh):
    n_row, n_col, n_dep = (mesh.shape[a] for a in ("row", "col", "depth"))

    def body(tensor, density, tensor_mask, density_mask):
        nu, mu_all, aux = tensor.shape
        sigma = density.shape[1]
        mu, q_dev, per_dev = mu_all // n_row, aux // n_col, sigma // n_dep
        chunks, hops, plane, width = mu // MC, n_dep // 2, nu * n_row * n_col, MC * (aux // n_col)
        vmem, smem = pl.BlockSpec(memory_space=pltpu.VMEM), pl.BlockSpec(memory_space=pltpu.SMEM)
        return pl.pallas_call(
            functools.partial(kernel, n_row, n_col, n_dep),
            out_shape=pltpu.VMEM((per_dev, mu, q_dev), BF),
            in_specs=[pl.BlockSpec(memory_space=pl.ANY), vmem, smem, smem],
            out_specs=vmem,
            scratch_shapes=[
                pltpu.VMEM((nu, n_row, GROUP, aux), BF),
                pltpu.VMEM((n_row, n_col, nu * GROUP, q_dev), F32),
                pltpu.VMEM((chunks, n_row, n_col, nu, width), BF),
                pltpu.VMEM((chunks, plane, width), BF),
                pltpu.VMEM((chunks, hops, per_dev, width), BF),
                pltpu.VMEM((chunks, hops, per_dev, width), BF),
                pltpu.VMEM((chunks, per_dev, width), BF),
                pltpu.VMEM((n_dep, nu, per_dev), BF),
                pltpu.VMEM((n_dep, plane, per_dev), BF),
                pltpu.VMEM((n_dep, per_dev, plane), BF),
                pltpu.VMEM((per_dev * GROUP, q_dev), F32),
                pltpu.SemaphoreType.DMA,
                pltpu.SemaphoreType.DMA((n_dep,)),
                pltpu.SemaphoreType.DMA((n_dep,)),
                pltpu.SemaphoreType.DMA((n_dep,)),
                pltpu.SemaphoreType.DMA((n_dep,)),
                pltpu.SemaphoreType.DMA((chunks,)),
                pltpu.SemaphoreType.DMA((chunks,)),
                pltpu.SemaphoreType.DMA((2, chunks)),
                pltpu.SemaphoreType.DMA((2, chunks, hops)),
            ],
            compiler_params=pltpu.CompilerParams(
                collective_id=0, has_side_effects=True, vmem_limit_bytes=54 << 20
            ),
        )(
            tensor.reshape(nu, n_row, mu, aux),
            density,
            tensor_mask.transpose(1, 2, 0),
            density_mask.T,
        )

    placed = (P(("row", "col", "depth"), None, None), P(("row", "col", "depth"), None), P(), P())
    return jax.shard_map(
        body, mesh=mesh, in_specs=placed, out_specs=P("depth", "row", "col"), check_vma=False
    )
```

```python
import functools

import jax
import jax.numpy as jnp
from jax import lax
from jax.experimental import pallas as pl
from jax.experimental.pallas import tpu as pltpu
from jax.sharding import PartitionSpec as P

BLK = 64
MESH = pl.DeviceIdType.MESH
MC = 4
GROUP = 16
LEAD = 2
BF, F32 = jnp.bfloat16, jnp.float32


def kernel(
    n_row, n_col, n_dep, tensor, density, tmask, dmask, out,
    raw, wide, ready, cols, down, up, first, own_den, den, den_t, total,
    load_sem, den_send, den_recv, sib_send, sib_recv, x_send, x_recv, z_send, z_recv,
):
    nu, _, mu, aux = tensor.shape
    per_dev = den.shape[2]
    half_rows = per_dev // 2
    q_dev = aux // n_col
    chunks = mu // MC
    per_group = GROUP // MC
    hops = n_dep // 2
    peers = n_row * n_col
    row, col, dep = lax.axis_index("row"), lax.axis_index("col"), lax.axis_index("depth")
    me = row * n_col + col
    left, right = lax.rem(dep + n_dep - 1, n_dep), lax.rem(dep + 1, n_dep)
    nu_block = lax.div((me * n_dep + dep) * nu, BLK)
    low = lax.broadcasted_iota(jnp.int32, (nu, 128), 1) < BLK
    mine = pl.ds(pl.multiple_of(me * nu, nu), nu)
    same_core = pl.ds(pl.multiple_of(row * n_col * nu, n_col * nu), n_col * nu)

    def peer(p):
        off = lax.rem(lax.div(p, 2) * 7, n_col)
        pr = lax.rem(row + lax.rem(p, 2), 2)
        y = lax.rem(lax.div(col, 4) + lax.div(off, 4), 4)
        x = lax.rem(lax.rem(col, 4) + lax.rem(off, 4), 4)
        return pr, y * 4 + x


    def load(g):
        return pltpu.make_async_copy(tensor.at[:, :, pl.ds(pl.multiple_of(g * GROUP, GROUP), GROUP), :], raw, load_sem)

    def widen(g):
        load(g).wait()

        @pl.loop(0, n_col)
        def _(c):
            lanes = pl.ds(pl.multiple_of(c * q_dev, q_dev), q_dev)
            for h in range(n_row):
                a = tmask[h, 2 * c, nu_block].astype(F32)
                b = tmask[h, 2 * c + 1, nu_block].astype(F32)
                keep = jnp.where(low, a, b)[:1][None]
                part = raw[:, h, :, lanes].astype(F32) * keep
                wide[h, c] = part.reshape(nu * GROUP, q_dev)

    def arrange(k):
        at = lax.rem(k, per_group) * MC

        @pl.loop(0, n_col)
        def _(c):
            for h in range(n_row):
                for j in range(MC):
                    ready[k, h, c, :, j * q_dev : (j + 1) * q_dev] = wide[
                        h, c, pl.ds(at + j, nu, stride=GROUP), :
                    ].astype(BF)

    def send(k):
        pltpu.make_async_copy(ready.at[k, row, col], cols.at[k, mine], x_recv.at[k]).start()

        @pl.loop(1, peers)
        def _(p):
            pr, pc = peer(p)
            pltpu.make_async_remote_copy(
                ready.at[k, pr, pc], cols.at[k, mine], x_send.at[k], x_recv.at[k],
                device_id=(pr, pc, dep), device_id_type=MESH,
            ).start()

    def prepare(k):
        @pl.when(lax.rem(k, per_group) == 0)
        def _():
            g = lax.div(k, per_group)
            widen(g)

            @pl.when(g + 1 < mu // GROUP)
            def _():
                load(g + 1).start()

        arrange(k)
        send(k)


    aheads = [hops] + [s * a for a in range(hops - 1, 0, -1) for s in (1, -1)] + [0]
    needs = [[0]] + [[2 * t - 1, 2 * t] for t in range(1, hops)] + [[n_dep - 1]]

    def block_of(ahead):
        return lax.rem(dep + ahead + n_dep, n_dep)

    def send_den(n):
        b = block_of(aheads[n])
        pltpu.make_async_copy(own_den.at[b], den.at[b, mine], den_recv.at[n]).start()

        @pl.loop(1, n_col)
        def _(p):
            _, pc = peer(2 * p)
            pltpu.make_async_remote_copy(
                own_den.at[b], den.at[b, mine], den_send.at[n], den_recv.at[n],
                device_id=(row, pc, dep), device_id_type=MESH,
            ).start()

    def sibling(n):
        part = den.at[block_of(aheads[n]), same_core]
        return pltpu.make_async_remote_copy(
            part, part, sib_send.at[n], sib_recv.at[n], device_id=(1 - row, col, dep), device_id_type=MESH
        )

    def share_den(n):
        part = den.at[block_of(aheads[n]), same_core]
        pltpu.make_async_copy(part, part, den_recv.at[n]).wait()
        sibling(n).start()

    def turn_den(n):
        b = block_of(aheads[n])
        sibling(n).wait_recv()
        den_t[b] = den[b].astype(F32).T.astype(BF)


    def product(k, ahead):
        return jnp.dot(den_t[block_of(ahead)], cols[k], preferred_element_type=F32)

    ways = ((down, right, 1), (up, left, -1))

    def hop(w, k, t):
        buf, other, _ = ways[w]
        rows = pl.ds(w * half_rows, half_rows) if t == 0 else slice(None)
        src = first.at[k, rows] if t == 0 else buf.at[k, t - 1]
        return pltpu.make_async_remote_copy(
            src, buf.at[k, t, rows], z_send.at[w, k], z_recv.at[w, k, t],
            device_id=(row, col, other), device_id_type=MESH,
        )

    def sent(k):
        rest = pl.ds(0, (peers - 1) * nu)
        pltpu.make_async_copy(cols.at[k, rest], cols.at[k, rest], x_send.at[k]).wait()
        rest = pl.ds(0, hops * per_dev - half_rows)
        for w in range(2):
            pltpu.make_async_copy(cols.at[k, rest], cols.at[k, rest], z_send.at[w, k]).wait()

    def stage(k, t):
        if t == 0:
            pltpu.make_async_copy(cols.at[k], cols.at[k], x_recv.at[k]).wait()
            first[k] = product(k, hops).astype(BF)
            for w in range(2):
                hop(w, k, 0).start()
        elif t < hops:
            for w in range(2):
                buf, _, sign = ways[w]
                mult = product(k, sign * (hops - t))
                hop(w, k, t - 1).wait_recv()
                if t == 1:
                    lo, hi = slice(0, half_rows), slice(half_rows, per_dev)
                    got, fresh = (lo, hi) if w == 0 else (hi, lo)
                    buf[k, 0, got] = (mult[got] + buf[k, 0, got].astype(F32)).astype(BF)
                    buf[k, 0, fresh] = mult[fresh].astype(BF)
                else:
                    buf[k, t - 1] = (mult + buf[k, t - 1].astype(F32)).astype(BF)
                hop(w, k, t).start()
        else:
            mult = product(k, 0)
            for w in range(2):
                hop(w, k, t - 1).wait_recv()
            mult = mult + down[k, t - 1].astype(F32) + up[k, t - 1].astype(F32)
            at = lax.rem(k, per_group) * MC
            for j in range(MC):
                total[pl.ds(at + j, per_dev, stride=GROUP), :] = mult[:, j * q_dev : (j + 1) * q_dev]

            @pl.when(lax.rem(k, per_group) == per_group - 1)
            def _():
                g = pl.ds(pl.multiple_of(lax.div(k, per_group) * GROUP, GROUP), GROUP)

                @pl.loop(0, per_dev // 16)
                def _(s):
                    part = total[pl.ds(pl.multiple_of(s * 16 * GROUP, 16 * GROUP), 16 * GROUP), :]
                    out[pl.ds(s * 16, 16), g, :] = part.reshape(16, GROUP, q_dev).astype(BF)

            @pl.when(k > 0)
            def _():
                sent(k - 1)

    load(0).start()
    barrier = pltpu.get_barrier_semaphore()

    @pl.loop(1, peers)
    def _(p):
        pr, pc = peer(p)
        pl.semaphore_signal(barrier, inc=1, device_id=(pr, pc, dep), device_id_type=MESH)

    pl.semaphore_signal(barrier, inc=1, device_id=(row, col, left), device_id_type=MESH)
    pl.semaphore_signal(barrier, inc=1, device_id=(row, col, right), device_id_type=MESH)
    for j in range(n_dep * per_dev // 128):
        a = dmask[2 * j, nu_block].astype(F32)
        b = dmask[2 * j + 1, nu_block].astype(F32)
        at = slice(j * 128 % per_dev, j * 128 % per_dev + 128)
        own_den[j * 128 // per_dev, :, at] = (
            density[:, j * 128 : (j + 1) * 128].astype(F32) * jnp.where(low, a, b)
        ).astype(BF)
    pl.semaphore_wait(barrier, peers + 1)

    for n in needs[0] + needs[1]:
        send_den(n)
    widen(0)
    load(1).start()
    for k in range(LEAD):
        arrange(k)
        send(k)
    for n in needs[0]:
        share_den(n)

    @pl.loop(0, hops + 1)
    def _(i):
        for t in range(hops, -1, -1):
            if t == 0:
                for s in range(LEAD, hops + 1):
                    @pl.when(i == s - LEAD)
                    def _(s=s):
                        for n in needs[s]:
                            send_den(n)

                @pl.when(i + LEAD < chunks)
                def _():
                    prepare(i + LEAD)

            @pl.when(i == t)
            def _(t=t):
                for n in needs[t]:
                    turn_den(n)

            @pl.when((i - t >= 0) & (i - t < chunks))
            def _(t=t):
                stage(i - t, t)

        for s in range(1, hops + 1):
            @pl.when(i == s - 1)
            def _(s=s):
                for n in needs[s]:
                    share_den(n)

    @pl.loop(hops + 1, chunks + hops)
    def _(i):
        for t in range(hops + 1):
            if t == 0:
                @pl.when(i + LEAD < chunks)
                def _():
                    prepare(i + LEAD)

            @pl.when((i - t >= 0) & (i - t < chunks))
            def _(t=t):
                stage(i - t, t)

    sent(chunks - 1)
    rest = pl.ds(0, (n_col - 1) * nu)
    for n in range(n_dep):
        pltpu.make_async_copy(den.at[0, rest], den.at[0, rest], den_send.at[n]).wait()
        sibling(n).wait_send()


def solution(mesh):
    n_row, n_col, n_dep = (mesh.shape[a] for a in ("row", "col", "depth"))

    def body(tensor, density, tensor_mask, density_mask):
        nu, mu_all, aux = tensor.shape
        sigma = density.shape[1]
        mu, q_dev, per_dev = mu_all // n_row, aux // n_col, sigma // n_dep
        chunks, hops, plane, width = mu // MC, n_dep // 2, nu * n_row * n_col, MC * (aux // n_col)
        vmem, smem = pl.BlockSpec(memory_space=pltpu.VMEM), pl.BlockSpec(memory_space=pltpu.SMEM)
        return pl.pallas_call(
            functools.partial(kernel, n_row, n_col, n_dep),
            out_shape=pltpu.VMEM((per_dev, mu, q_dev), BF),
            in_specs=[pl.BlockSpec(memory_space=pl.ANY), vmem, smem, smem],
            out_specs=vmem,
            scratch_shapes=[
                pltpu.VMEM((nu, n_row, GROUP, aux), BF),
                pltpu.VMEM((n_row, n_col, nu * GROUP, q_dev), F32),
                pltpu.VMEM((chunks, n_row, n_col, nu, width), BF),
                pltpu.VMEM((chunks, plane, width), BF),
                pltpu.VMEM((chunks, hops, per_dev, width), BF),
                pltpu.VMEM((chunks, hops, per_dev, width), BF),
                pltpu.VMEM((chunks, per_dev, width), BF),
                pltpu.VMEM((n_dep, nu, per_dev), BF),
                pltpu.VMEM((n_dep, plane, per_dev), BF),
                pltpu.VMEM((n_dep, per_dev, plane), BF),
                pltpu.VMEM((per_dev * GROUP, q_dev), F32),
                pltpu.SemaphoreType.DMA,
                pltpu.SemaphoreType.DMA((n_dep,)),
                pltpu.SemaphoreType.DMA((n_dep,)),
                pltpu.SemaphoreType.DMA((n_dep,)),
                pltpu.SemaphoreType.DMA((n_dep,)),
                pltpu.SemaphoreType.DMA((chunks,)),
                pltpu.SemaphoreType.DMA((chunks,)),
                pltpu.SemaphoreType.DMA((2, chunks)),
                pltpu.SemaphoreType.DMA((2, chunks, hops)),
            ],
            compiler_params=pltpu.CompilerParams(
                collective_id=0, has_side_effects=True, vmem_limit_bytes=54 << 20
            ),
        )(
            tensor.reshape(nu, n_row, mu, aux),
            density,
            tensor_mask.transpose(1, 2, 0),
            density_mask.T,
        )

    placed = (P(("row", "col", "depth"), None, None), P(("row", "col", "depth"), None), P(), P())
    return jax.shard_map(
        body, mesh=mesh, in_specs=placed, out_specs=P("depth", "row", "col"), check_vma=False
    )
```

```python
import functools

import jax
import jax.numpy as jnp
from jax import lax
from jax.experimental import pallas as pl
from jax.experimental.pallas import tpu as pltpu
from jax.sharding import PartitionSpec as P

BLK = 64
MESH = pl.DeviceIdType.MESH
MC = 4
GROUP = 16
LEAD = 2
BF, F32 = jnp.bfloat16, jnp.float32


def kernel(
    n_row, n_col, n_dep, tensor, density, tmask, dmask, out,
    raw, wide, ready, cols, down, up, first, own_den, den, den_t, total,
    load_sem, den_send, den_recv, sib_send, sib_recv, x_send, x_recv, z_send, z_recv,
):
    nu, _, mu, aux = tensor.shape
    per_dev = den.shape[2]
    half_rows = per_dev // 2
    q_dev = aux // n_col
    chunks = mu // MC
    per_group = GROUP // MC
    hops = n_dep // 2
    peers = n_row * n_col
    row, col, dep = lax.axis_index("row"), lax.axis_index("col"), lax.axis_index("depth")
    me = row * n_col + col
    left, right = lax.rem(dep + n_dep - 1, n_dep), lax.rem(dep + 1, n_dep)
    nu_block = lax.div((me * n_dep + dep) * nu, BLK)
    low = lax.broadcasted_iota(jnp.int32, (nu, 128), 1) < BLK
    mine = pl.ds(pl.multiple_of(me * nu, nu), nu)
    same_core = pl.ds(pl.multiple_of(row * n_col * nu, n_col * nu), n_col * nu)

    def peer(p):
        off = lax.rem(lax.div(p, 2) * 7, n_col)
        pr = lax.rem(row + lax.rem(p, 2), 2)
        y = lax.rem(lax.div(col, 4) + lax.div(off, 4), 4)
        x = lax.rem(lax.rem(col, 4) + lax.rem(off, 4), 4)
        return pr, y * 4 + x


    def load(g):
        return pltpu.make_async_copy(tensor.at[:, :, pl.ds(pl.multiple_of(g * GROUP, GROUP), GROUP), :], raw, load_sem)

    def widen(g):
        load(g).wait()

        @pl.loop(0, n_col)
        def _(c):
            lanes = pl.ds(pl.multiple_of(c * q_dev, q_dev), q_dev)
            for h in range(n_row):
                a = tmask[h, 2 * c, nu_block].astype(F32)
                b = tmask[h, 2 * c + 1, nu_block].astype(F32)
                keep = jnp.where(low, a, b)[:1][None]
                part = raw[:, h, :, lanes].astype(F32) * keep
                wide[h, c, : nu * GROUP] = part.reshape(nu * GROUP, q_dev)

    def arrange(k):
        at = lax.rem(k, per_group) * MC

        @pl.loop(0, n_col)
        def _(c):
            for h in range(n_row):
                for j in range(MC):
                    ready[k, h, c, :, j * q_dev : (j + 1) * q_dev] = wide[
                        h, c, pl.ds(at + j, nu, stride=GROUP), :
                    ].astype(BF)

    def send(k):
        pltpu.make_async_copy(ready.at[k, row, col], cols.at[k, mine], x_recv.at[k]).start()

        @pl.loop(1, peers)
        def _(p):
            pr, pc = peer(p)
            pltpu.make_async_remote_copy(
                ready.at[k, pr, pc], cols.at[k, mine], x_send.at[k], x_recv.at[k],
                device_id=(pr, pc, dep), device_id_type=MESH,
            ).start()

    def prepare(k):
        @pl.when(lax.rem(k, per_group) == 0)
        def _():
            g = lax.div(k, per_group)
            widen(g)

            @pl.when(g + 1 < mu // GROUP)
            def _():
                load(g + 1).start()

        arrange(k)
        send(k)


    aheads = [hops] + [s * a for a in range(hops - 1, 0, -1) for s in (1, -1)] + [0]
    needs = [[0]] + [[2 * t - 1, 2 * t] for t in range(1, hops)] + [[n_dep - 1]]

    def block_of(ahead):
        return lax.rem(dep + ahead + n_dep, n_dep)

    def send_den(n):
        b = block_of(aheads[n])
        pltpu.make_async_copy(own_den.at[b], den.at[b, mine], den_recv.at[n]).start()

        @pl.loop(1, n_col)
        def _(p):
            _, pc = peer(2 * p)
            pltpu.make_async_remote_copy(
                own_den.at[b], den.at[b, mine], den_send.at[n], den_recv.at[n],
                device_id=(row, pc, dep), device_id_type=MESH,
            ).start()

    def sibling(n):
        part = den.at[block_of(aheads[n]), same_core]
        return pltpu.make_async_remote_copy(
            part, part, sib_send.at[n], sib_recv.at[n], device_id=(1 - row, col, dep), device_id_type=MESH
        )

    def share_den(n):
        part = den.at[block_of(aheads[n]), same_core]
        pltpu.make_async_copy(part, part, den_recv.at[n]).wait()
        sibling(n).start()

    def turn_den(n):
        b = block_of(aheads[n])
        sibling(n).wait_recv()
        den_t[b] = den[b].astype(F32).T.astype(BF)


    def product(k, ahead):
        return jnp.dot(den_t[block_of(ahead)], cols[k], preferred_element_type=F32)

    ways = ((down, right, 1), (up, left, -1))

    def hop(w, k, t):
        buf, other, _ = ways[w]
        rows = pl.ds(w * half_rows, half_rows) if t == 0 else slice(None)
        src = first.at[k, rows] if t == 0 else buf.at[k, t - 1]
        return pltpu.make_async_remote_copy(
            src, buf.at[k, t, rows], z_send.at[w, k], z_recv.at[w, k, t],
            device_id=(row, col, other), device_id_type=MESH,
        )

    def sent(k):
        rest = pl.ds(0, (peers - 1) * nu)
        pltpu.make_async_copy(cols.at[k, rest], cols.at[k, rest], x_send.at[k]).wait()
        rest = pl.ds(0, hops * per_dev - half_rows)
        for w in range(2):
            pltpu.make_async_copy(cols.at[k, rest], cols.at[k, rest], z_send.at[w, k]).wait()

    def stage(k, t):
        if t == 0:
            pltpu.make_async_copy(cols.at[k], cols.at[k], x_recv.at[k]).wait()
            first[k] = product(k, hops).astype(BF)
            for w in range(2):
                hop(w, k, 0).start()
        elif t < hops:
            for w in range(2):
                buf, _, sign = ways[w]
                mult = product(k, sign * (hops - t))
                hop(w, k, t - 1).wait_recv()
                if t == 1:
                    lo, hi = slice(0, half_rows), slice(half_rows, per_dev)
                    got, fresh = (lo, hi) if w == 0 else (hi, lo)
                    buf[k, 0, got] = (mult[got] + buf[k, 0, got].astype(F32)).astype(BF)
                    buf[k, 0, fresh] = mult[fresh].astype(BF)
                else:
                    buf[k, t - 1] = (mult + buf[k, t - 1].astype(F32)).astype(BF)
                hop(w, k, t).start()
        else:
            mult = product(k, 0)
            for w in range(2):
                hop(w, k, t - 1).wait_recv()
            mult = mult + down[k, t - 1].astype(F32) + up[k, t - 1].astype(F32)
            at = lax.rem(k, per_group) * MC
            for j in range(MC):
                total[pl.ds(at + j, per_dev, stride=GROUP), :] = mult[:, j * q_dev : (j + 1) * q_dev]

            @pl.when(lax.rem(k, per_group) == per_group - 1)
            def _():
                g = pl.ds(pl.multiple_of(lax.div(k, per_group) * GROUP, GROUP), GROUP)

                @pl.loop(0, per_dev // 16)
                def _(s):
                    part = total[pl.ds(pl.multiple_of(s * 16 * GROUP, 16 * GROUP), 16 * GROUP), :]
                    out[pl.ds(s * 16, 16), g, :] = part.reshape(16, GROUP, q_dev).astype(BF)

            @pl.when(k > 0)
            def _():
                sent(k - 1)

    load(0).start()
    barrier = pltpu.get_barrier_semaphore()

    @pl.loop(1, peers)
    def _(p):
        pr, pc = peer(p)
        pl.semaphore_signal(barrier, inc=1, device_id=(pr, pc, dep), device_id_type=MESH)

    pl.semaphore_signal(barrier, inc=1, device_id=(row, col, left), device_id_type=MESH)
    pl.semaphore_signal(barrier, inc=1, device_id=(row, col, right), device_id_type=MESH)
    for j in range(n_dep * per_dev // 128):
        a = dmask[2 * j, nu_block].astype(F32)
        b = dmask[2 * j + 1, nu_block].astype(F32)
        at = slice(j * 128 % per_dev, j * 128 % per_dev + 128)
        own_den[j * 128 // per_dev, :, at] = (
            density[:, j * 128 : (j + 1) * 128].astype(F32) * jnp.where(low, a, b)
        ).astype(BF)
    pl.semaphore_wait(barrier, peers + 1)

    for n in needs[0] + needs[1]:
        send_den(n)
    widen(0)
    load(1).start()
    for k in range(LEAD):
        arrange(k)
        send(k)
    for n in needs[0]:
        share_den(n)

    @pl.loop(0, hops + 1)
    def _(i):
        for t in range(hops, -1, -1):
            if t == 0:
                for s in range(LEAD, hops + 1):
                    @pl.when(i == s - LEAD)
                    def _(s=s):
                        for n in needs[s]:
                            send_den(n)

                @pl.when(i + LEAD < chunks)
                def _():
                    prepare(i + LEAD)

            @pl.when(i == t)
            def _(t=t):
                for n in needs[t]:
                    turn_den(n)

            @pl.when((i - t >= 0) & (i - t < chunks))
            def _(t=t):
                stage(i - t, t)

        for s in range(1, hops + 1):
            @pl.when(i == s - 1)
            def _(s=s):
                for n in needs[s]:
                    share_den(n)

    rest = pl.ds(0, (n_col - 1) * nu)
    for n in range(n_dep):
        pltpu.make_async_copy(den.at[0, rest], den.at[0, rest], den_send.at[n]).wait()
        sibling(n).wait_send()

    @pl.loop(hops + 1, chunks + hops)
    def _(i):
        for t in range(hops + 1):
            if t == 0:
                @pl.when(i + LEAD < chunks)
                def _():
                    prepare(i + LEAD)

            @pl.when((i - t >= 0) & (i - t < chunks))
            def _(t=t):
                stage(i - t, t)

    sent(chunks - 1)


def solution(mesh):
    n_row, n_col, n_dep = (mesh.shape[a] for a in ("row", "col", "depth"))

    def body(tensor, density, tensor_mask, density_mask):
        nu, mu_all, aux = tensor.shape
        sigma = density.shape[1]
        mu, q_dev, per_dev = mu_all // n_row, aux // n_col, sigma // n_dep
        chunks, hops, plane, width = mu // MC, n_dep // 2, nu * n_row * n_col, MC * (aux // n_col)
        vmem, smem = pl.BlockSpec(memory_space=pltpu.VMEM), pl.BlockSpec(memory_space=pltpu.SMEM)
        return pl.pallas_call(
            functools.partial(kernel, n_row, n_col, n_dep),
            out_shape=pltpu.VMEM((per_dev, mu, q_dev), BF),
            in_specs=[pl.BlockSpec(memory_space=pl.ANY), vmem, smem, smem],
            out_specs=vmem,
            scratch_shapes=[
                pltpu.VMEM((nu, n_row, GROUP, aux), BF),
                pltpu.VMEM((n_row, n_col, (nu + 1) * GROUP, q_dev), F32),
                pltpu.VMEM((chunks, n_row, n_col, nu, width), BF),
                pltpu.VMEM((chunks, plane, width), BF),
                pltpu.VMEM((chunks, hops, per_dev, width), BF),
                pltpu.VMEM((chunks, hops, per_dev, width), BF),
                pltpu.VMEM((chunks, per_dev, width), BF),
                pltpu.VMEM((n_dep, nu, per_dev), BF),
                pltpu.VMEM((n_dep, plane, per_dev), BF),
                pltpu.VMEM((n_dep, per_dev, plane), BF),
                pltpu.VMEM(((per_dev + 1) * GROUP, q_dev), F32),
                pltpu.SemaphoreType.DMA,
                pltpu.SemaphoreType.DMA((n_dep,)),
                pltpu.SemaphoreType.DMA((n_dep,)),
                pltpu.SemaphoreType.DMA((n_dep,)),
                pltpu.SemaphoreType.DMA((n_dep,)),
                pltpu.SemaphoreType.DMA((chunks,)),
                pltpu.SemaphoreType.DMA((chunks,)),
                pltpu.SemaphoreType.DMA((2, chunks)),
                pltpu.SemaphoreType.DMA((2, chunks, hops)),
            ],
            compiler_params=pltpu.CompilerParams(
                collective_id=0, has_side_effects=True, vmem_limit_bytes=54 << 20
            ),
        )(
            tensor.reshape(nu, n_row, mu, aux),
            density,
            tensor_mask.transpose(1, 2, 0),
            density_mask.T,
        )

    placed = (P(("row", "col", "depth"), None, None), P(("row", "col", "depth"), None), P(), P())
    return jax.shard_map(
        body, mesh=mesh, in_specs=placed, out_specs=P("depth", "row", "col"), check_vma=False
    )
```
